32 devices in a mesh: grp: 4 (over y, x), dev: 8 (over z, core).
Axes of the slice: x: 2, y: 2, z: 4, core: 2. Of those that a mesh axis runs over, the one named last changes fastest.
Arguments:
- block_values: bfloat16 [384, 9, 128, 128], P(('grp', 'dev')), may hold values from -0.1875 to 0.1875
- block_columns: int32 [384, 9], P(('grp', 'dev')), may hold values from 0 to 17, as said below
- tentative: bfloat16 [384, 128, 128], P(('grp', 'dev')), may hold values from -1.1953125 to 1.1953125
- inverse_diagonal: bfloat16 [384, 128, 128], P(('grp', 'dev')), may hold values from -0.5 to 0.5
- aggregate: int32 [384], P(('grp', 'dev')), may hold values from 0 to 1, as said below
- ghost_rows: int32 [32, 2, 3], P(('grp', 'dev')), may hold values from 0 to 11, as said below
- damping: float32 [1], replicated, may hold values from 0.5 to 0.8
Outputs:
- coarse_op: bfloat16 [64, 128, 1792], P(('grp', 'dev'))
The draws below stay inside these ranges and needn't reach their ends.
Inputs may be any that keep to these rules, and one draw needn't show every extreme that they name: `block_columns`: in part n, row r names its own row r first; the 9 entries of a row differ; entries from 12 to 14 never stand in the first part, entries from 15 on never in the last. `aggregate`: each of the 2 aggregates of a part holds one or more of its rows. `ghost_rows`: the 3 rows of each list differ.
All inputs are finite; a program needn't handle non-finite values.
Results may differ from the reference program's by a relative error of at most 0.0068.
Values may be sent and summed in bfloat16 or wider, within the bound.
A program may use at most 64 MiB of HBM per device.

```python
import jax
import jax.numpy as jnp
from jax import lax

B = 128
K = 9
CA = 2
R = 12
S = 3
NB = 384
N_GRP = 4
N_DEV = 8


def draw_block_columns(key, part):
    key = jax.random.fold_in(key, 11)
    devices = N_GRP * N_DEV
    choices_all = R + 2 * S
    candidate = jnp.arange(choices_all, dtype=jnp.int32)[None, None, :]
    device_index = jnp.arange(devices, dtype=jnp.int32)[:, None, None]
    row_index = jnp.arange(R, dtype=jnp.int32)[None, :, None]
    left_ghost = (candidate >= R) & (candidate < R + S)
    right_ghost = candidate >= R + S
    usable = (candidate != row_index) & ~(left_ghost & (device_index == 0)) & ~(right_ghost & (device_index == devices - 1))
    scores = jax.random.randint(key, (devices, R, choices_all), 0, 1 << 20) * choices_all + candidate
    scores = jnp.where(usable, scores, -1)
    picked = lax.top_k(scores, K - 1)[0] % choices_all
    first = jnp.broadcast_to(row_index, (devices, R, 1))
    return jnp.concatenate([first, picked], axis=2).reshape(devices * R, K).astype(jnp.int32)


def draw_aggregate(key, part):
    devices = N_GRP * N_DEV
    keys_all = jax.random.split(jax.random.fold_in(key, 23), devices)
    orders = jax.vmap(lambda single: jax.random.permutation(single, R))(keys_all)
    extra = jax.random.randint(jax.random.fold_in(key, 24), (devices, R), 0, CA)
    position = jnp.arange(R, dtype=jnp.int32)[None, :]
    labels = jnp.where(position < CA, position, extra)
    inverse = jnp.argsort(orders, axis=1)
    return jnp.take_along_axis(labels, inverse, axis=1).reshape(devices * R).astype(jnp.int32)


def draw_ghost_rows(key, part):
    devices = N_GRP * N_DEV
    keys_all = jax.random.split(jax.random.fold_in(key, 37), devices * 2)
    orders = jax.vmap(lambda single: jax.random.permutation(single, R))(keys_all)
    return orders[:, :S].reshape(devices, 2, S).astype(jnp.int32)


def shard_levels(key, shape, cuts, least, top_value):
    def one(axis_at, shards_of):
        steps = jax.random.uniform(jax.random.fold_in(jax.random.fold_in(key, 6), axis_at), (shards_of,), jnp.float32, least / len(cuts), top_value / len(cuts))
        return jnp.repeat(jnp.exp(steps), shape[axis_at] // shards_of).reshape((-1,) + (1,) * (len(shape) - axis_at - 1))

    factor_of = one(*cuts[0])
    for cut in cuts[1:]:
        factor_of = factor_of * one(*cut)
    return factor_of


def normal_values(own_key, dims, scale, limit, cuts=(), kind=jnp.bfloat16):
    entries = scale * jax.random.normal(own_key, dims, jnp.float32)
    if cuts:
        entries = entries * shard_levels(own_key, dims, cuts, -0.22, 0.18)
    return jnp.clip(entries, -limit, limit).astype(kind)


def setup_inputs(seed: int = 0) -> dict:
    splits = jax.random.split(jax.random.key(seed), 8)
    return {
        "block_values": normal_values(splits[0], (NB, K, B, B), (K * B) ** -0.5, 0.1875, ((0, 32),)),
        "block_columns": draw_block_columns(jax.random.fold_in(splits[7], 71), 0),
        "tentative": normal_values(splits[2], (NB, B, B), 0.2, 1.1953125, ((0, 32),)),
        "inverse_diagonal": normal_values(splits[3], (NB, B, B), B ** -0.5, 0.5, ((0, 32),)),
        "aggregate": draw_aggregate(jax.random.fold_in(splits[7], 71), 0),
        "ghost_rows": draw_ghost_rows(jax.random.fold_in(splits[7], 71), 0),
        "damping": jnp.clip(jax.random.uniform(splits[6], (1,), jnp.float32, 0.5, 0.8), 0.5, 0.8),
    }


def place_own(tentative, aggregate):
    aggregate_mask = aggregate[:, None] == jnp.arange(CA, dtype=jnp.int32)[None, :]
    spread = jnp.where(aggregate_mask[:, None, :, None], tentative[:, :, None, :], jnp.zeros((), tentative.dtype))
    return spread.reshape(tentative.shape[0], tentative.shape[1], CA * tentative.shape[2])


def side_of(columns):
    return jnp.where(columns < R, 1, jnp.where(columns < R + S, 0, 2)).astype(jnp.int32)


def by_side(product_term, column_side, block_span):
    left_pad = jnp.pad(product_term, ((0, 0), (0, 0), (0, 2 * block_span)))
    middle_pad = jnp.pad(product_term, ((0, 0), (0, 0), (block_span, block_span)))
    right_pad = jnp.pad(product_term, ((0, 0), (0, 0), (2 * block_span, 0)))
    side_index = column_side[:, None, None]
    return jnp.where(side_index == 0, left_pad, jnp.where(side_index == 1, middle_pad, right_pad))


def assemble(values, columns, column_side, lookup, block_span):
    start = jnp.zeros((values.shape[0], B, lookup.shape[2] + 2 * block_span), jnp.float32)

    def accumulate(slot_index, running_sum):
        column_now = lax.dynamic_index_in_dim(columns, slot_index, 1, keepdims=False)
        side_now = lax.dynamic_index_in_dim(column_side, slot_index, 1, keepdims=False)
        value_now = lax.dynamic_index_in_dim(values, slot_index, 1, keepdims=False)
        picked = jnp.take(lookup, column_now, axis=0)
        product_term = jnp.einsum("rab,rbc->rac", value_now.astype(jnp.float32), picked.astype(jnp.float32), precision=lax.Precision.HIGHEST)
        return running_sum + by_side(product_term, side_now, block_span)

    return lax.fori_loop(0, values.shape[1], accumulate, start)


def neighbours(shards):
    blank = jnp.zeros_like(shards[:1])
    return jnp.concatenate([blank, shards[:-1]], axis=0), jnp.concatenate([shards[1:], blank], axis=0)


def reference(block_values, block_columns, tentative, inverse_diagonal, aggregate, ghost_rows, damping):
    devices = N_GRP * N_DEV
    block_span = CA * B
    own_all = place_own(tentative, aggregate).reshape(devices, R, B, block_span)
    values_all = block_values.reshape(devices, R, K, B, B)
    columns_all = block_columns.reshape(devices, R, K)
    inverse_all = inverse_diagonal.reshape(devices, R, B, B)
    left_all, right_all = neighbours(own_all)

    def smooth_part(pieces):
        values, columns, ghost_lists, own_rows, left_rows, right_rows, inverse = pieces
        column_side = side_of(columns)
        lookup = jnp.concatenate([own_rows, jnp.take(left_rows, ghost_lists[0], axis=0), jnp.take(right_rows, ghost_lists[1], axis=0)], axis=0)
        smooth_sum = assemble(values, columns, column_side, lookup, block_span)
        smooth_half = lax.optimization_barrier(smooth_sum.astype(jnp.bfloat16))
        scaled = jnp.einsum("rab,rbc->rac", inverse.astype(jnp.float32), smooth_half.astype(jnp.float32), precision=lax.Precision.HIGHEST)
        own_wide = jnp.pad(own_rows, ((0, 0), (0, 0), (block_span, block_span))).astype(jnp.float32)
        return (own_wide - damping[0] * scaled).astype(jnp.bfloat16)

    prolong_all = lax.map(smooth_part, (values_all, columns_all, ghost_rows, own_all, left_all, right_all, inverse_all))
    left_prolong, right_prolong = neighbours(prolong_all)

    def galerkin_part(pieces):
        values, columns, ghost_lists, own_rows, left_rows, right_rows = pieces
        column_side = side_of(columns)
        lookup = jnp.concatenate([own_rows, jnp.take(left_rows, ghost_lists[0], axis=0), jnp.take(right_rows, ghost_lists[1], axis=0)], axis=0)
        applied = assemble(values, columns, column_side, lookup, block_span).astype(jnp.bfloat16)
        flat_prolong = own_rows.reshape(R * B, 3 * block_span).astype(jnp.float32)
        flat_applied = applied.reshape(R * B, 5 * block_span).astype(jnp.float32)
        return lax.dot_general(flat_prolong, flat_applied, (((0,), (0,)), ((), ())), precision=lax.Precision.HIGHEST)

    partial_rows = lax.map(galerkin_part, (values_all, columns_all, ghost_rows, prolong_all, left_prolong, right_prolong))
    blank = jnp.zeros_like(partial_rows[:1, :block_span])
    middle = partial_rows[:, block_span:2 * block_span]
    from_right = jnp.concatenate([partial_rows[1:, :block_span], blank], axis=0)
    from_left = jnp.concatenate([blank, partial_rows[:-1, 2 * block_span:]], axis=0)
    coarse = jnp.pad(middle, ((0, 0), (0, 0), (block_span, block_span)))
    coarse = coarse + jnp.pad(from_right, ((0, 0), (0, 0), (2 * block_span, 0)))
    coarse = coarse + jnp.pad(from_left, ((0, 0), (0, 0), (0, 2 * block_span)))
    return coarse.reshape(devices * CA, B, 7 * block_span).astype(jnp.bfloat16)
```

```python
import functools

import jax
import jax.numpy as jnp
from jax import lax
from jax.experimental import pallas as pl
from jax.experimental.pallas import tpu as pltpu
from jax.sharding import PartitionSpec as P

CA = 2
HEAD = 8
LANES = 128
META, TENT, MID, LEFT, RIGHT, PART = 0, 1, 2, 3, 4, 5
MESSAGES = 10


def dot(a, b):
    return jnp.dot(a, b, preferred_element_type=jnp.float32)


def kernel(
    n_grp,
    n_dev,
    damping_ref,
    meta_ref,
    meta_vec,
    values_hbm,
    tent_hbm,
    inv_hbm,
    out_hbm,
    a_raw,
    t_raw,
    d_raw,
    a_own,
    a_side,
    tt,
    stage_t,
    ghost_t,
    meta_in,
    meta_s,
    tg,
    p,
    stage_p,
    ghost_p,
    pt,
    ap,
    own_acc,
    part_send,
    part_recv,
    out_v,
    a_sem,
    local_sem,
    out_sem,
    send_sem,
    recv_sem,
):
    rows, slots, width, _ = values_hbm.shape
    listed = stage_t.shape[1]
    span = CA * width
    group = max(g for g in (1, 2, 3, 4) if rows % g == 0)
    chunk = group * width
    total = n_grp * n_dev
    me = lax.axis_index("grp") * n_dev + lax.axis_index("dev")
    has = (me > 0, me < total - 1)
    other = (lax.rem(me + (total - 1), total), lax.rem(me + 1, total))
    device = [(lax.div(o, n_dev), lax.rem(o, n_dev)) for o in other]

    def message(side, index, source, target):
        return pltpu.make_async_remote_copy(
            src_ref=source,
            dst_ref=target,
            send_sem=send_sem.at[side, index],
            recv_sem=recv_sem.at[1 - side, index],
            device_id=device[side],
            device_id_type=pl.DeviceIdType.MESH,
        )

    def meta_msg(side):
        return message(side, META, meta_vec.at[pl.ds(0, HEAD)], meta_in.at[1 - side])

    def tent_msg(side):
        return message(side, TENT, stage_t.at[side], ghost_t.at[1 - side])

    def p_msg(side, part):
        index = (LEFT, MID, RIGHT)[part]
        return message(side, index, stage_p.at[side, part], ghost_p.at[1 - side, part])

    def part_msg(side, column):
        return message(
            side, PART + column, part_send.at[side, column], part_recv.at[1 - side, column]
        )

    def both(action):
        for side in (0, 1):
            pl.when(has[side])(functools.partial(action, side))

    barrier = pltpu.get_barrier_semaphore()
    both(
        lambda side: pl.semaphore_signal(
            barrier, inc=1, device_id=device[side], device_id_type=pl.DeviceIdType.MESH
        )
    )

    def a_copy(r):
        return pltpu.make_async_copy(
            values_hbm.at[r], a_raw.at[r, pl.ds(0, slots)], a_sem.at[r]
        )

    t_copy = pltpu.make_async_copy(tent_hbm, t_raw, local_sem.at[0])
    d_copy = pltpu.make_async_copy(inv_hbm, d_raw, local_sem.at[1])
    t_copy.start()

    @pl.loop(0, rows)
    def _(r):
        a_copy(r).start()
        a_raw[r, slots] = jnp.zeros((width, width), a_raw.dtype)

    d_copy.start()
    for side in (0, 1):

        @pl.when(jnp.logical_not(has[side]))
        def _():
            tg[side] = jnp.zeros(tg.shape[1:], tg.dtype)
            ghost_p[side] = jnp.zeros(ghost_p.shape[1:], ghost_p.dtype)
            part_recv[side] = jnp.zeros(part_recv.shape[1:], part_recv.dtype)

    pl.semaphore_wait(barrier, has[0].astype(jnp.int32) + has[1].astype(jnp.int32))
    both(lambda side: meta_msg(side).start())

    def placed(block, coarse):
        wide = jnp.concatenate([block] * CA, axis=1)
        at = lax.broadcasted_iota(jnp.int32, wide.shape, 1) // width
        return jnp.where(at == jnp.full(wide.shape, coarse, jnp.int32), wide, 0).astype(block.dtype)

    t_copy.wait()

    @pl.loop(0, rows)
    def _(r):
        tt[pl.ds(pl.multiple_of(r * width, width), width), :] = placed(t_raw[r], meta_ref[2, r])

    def lists_in(side):
        meta_msg(1 - side).wait_recv()
        copy = pltpu.make_async_copy(meta_in.at[side], meta_s.at[side], local_sem.at[2 + side])
        copy.start()
        copy.wait()
        for s in range(listed):
            stage_t[side, s] = t_raw[meta_s[side, 1 - side, s]]
        tent_msg(side).start()

    both(lists_in)

    @pl.loop(0, rows)
    def _(r):
        a_copy(r).wait()

    @pl.loop(0, rows)
    def _(r):
        at = pl.ds(pl.multiple_of(r * width, width), width)
        for l in range(rows):
            a_own[at, l * width : (l + 1) * width] = a_raw[r, meta_ref[HEAD + r, l]]
        for side in (0, 1):
            for s in range(listed):
                a_side[side, at, s * width : (s + 1) * width] = a_raw[
                    r, meta_ref[HEAD + r, rows + side * listed + s]
                ]

    d_copy.wait()
    damping = damping_ref[0]

    def smooth(part, matrix, lookup, keep):
        @pl.loop(0, rows // group)
        def _(g):
            at = pl.ds(pl.multiple_of(g * chunk, chunk), chunk)
            half = dot(matrix[at, :], lookup[...]).astype(jnp.bfloat16)
            for i in range(group):
                r = g * group + i
                here = pl.ds(pl.multiple_of(r * width, width), width)
                scaled = damping * dot(d_raw[r], half[i * width : (i + 1) * width])
                if keep:
                    value = tt[here, :].astype(jnp.float32) - scaled
                else:
                    value = -scaled
                p[part, r] = value.astype(jnp.bfloat16)

    def send_p(part):
        def send(side):
            for s in range(listed):
                stage_p[side, part, s * width : (s + 1) * width, :] = p[
                    part, meta_s[side, 1 - side, s]
                ]
            p_msg(side, part).start()

        both(send)

    smooth(1, a_own, tt, True)
    send_p(1)

    def tent_in(side):
        tent_msg(1 - side).wait_recv()
        for s in range(listed):
            coarse = meta_s[side, 2, meta_ref[side, s]]
            tg[side, s * width : (s + 1) * width, :] = placed(ghost_t[side, s], coarse)

    both(tent_in)
    smooth(0, a_side.at[0], tg.at[0], False)
    send_p(0)
    smooth(2, a_side.at[1], tg.at[1], False)
    send_p(2)

    for part in range(3):

        @pl.loop(0, rows)
        def _(r):
            pt[part, r] = p[part, r].T

    def galerkin(column, terms):
        @pl.loop(0, rows // group)
        def _(g):
            at = pl.ds(pl.multiple_of(g * chunk, chunk), chunk)
            value = None
            for matrix, lookup in terms:
                term = dot(matrix[at, :], lookup[...].reshape(-1, span))
                value = term if value is None else value + term
            ap[at, :] = value.astype(jnp.bfloat16)

        def product(part):
            lhs = jnp.concatenate([pt[part, r] for r in range(rows)], axis=1)
            return dot(lhs, ap[...])

        for side, part in ((0, 0), (1, 2)):
            part_send[side, column] = product(part).astype(jnp.bfloat16)
            pl.when(has[side])(lambda: part_msg(side, column).start())
        own_acc[column] = product(1)

    def p_in(side, part):
        pl.when(has[side])(lambda: p_msg(1 - side, part).wait_recv())

    left, right = a_side.at[0], a_side.at[1]
    p_in(0, 1)
    galerkin(1, [(a_own, p.at[0]), (left, ghost_p.at[0, 1])])
    p_in(1, 1)
    galerkin(3, [(a_own, p.at[2]), (right, ghost_p.at[1, 1])])
    p_in(0, 0)
    galerkin(0, [(left, ghost_p.at[0, 0])])
    p_in(1, 2)
    galerkin(4, [(right, ghost_p.at[1, 2])])
    p_in(0, 2)
    p_in(1, 0)
    galerkin(2, [(a_own, p.at[1]), (left, ghost_p.at[0, 2]), (right, ghost_p.at[1, 0])])

    def out_copy(s):
        return pltpu.make_async_copy(
            out_v.at[s], out_hbm.at[:, :, pl.ds(s * span, span)], out_sem.at[s]
        )

    for s in (1, 5, 3, 0, 6, 2, 4):
        value = None
        if 0 <= s - 1 < 5:
            value = own_acc[s - 1]
        for side, column in ((0, s), (1, s - 2)):
            if 0 <= column < 5:
                pl.when(has[side])(lambda: part_msg(1 - side, column).wait_recv())
                term = part_recv[side, column].astype(jnp.float32)
                value = term if value is None else value + term
        out_v[s] = value.astype(jnp.bfloat16).reshape(CA, width, span)
        out_copy(s).start()

    def finish(side):
        meta_msg(side).wait_send()
        tent_msg(side).wait_send()
        for part in range(3):
            p_msg(side, part).wait_send()
        for column in range(5):
            part_msg(side, column).wait_send()

    both(finish)
    for s in range(7):
        out_copy(s).wait()


def shards(
    n_grp,
    n_dev,
    block_values,
    block_columns,
    tentative,
    inverse_diagonal,
    aggregate,
    ghost_rows,
    damping,
):
    rows, slots = block_columns.shape
    width = tentative.shape[1]
    listed = ghost_rows.shape[2]
    lookups = rows + 2 * listed
    span = CA * width
    slot = jnp.arange(slots, dtype=jnp.int32)[None, :, None] - slots
    match = block_columns[:, :, None] == jnp.arange(LANES, dtype=jnp.int32)[None, None, :]
    place = jnp.sum(jnp.where(match, slot, 0), axis=1, dtype=jnp.int32) + slots
    head = jnp.concatenate(
        [
            jnp.pad(ghost_rows[0], ((0, 0), (0, LANES - listed))),
            jnp.pad(aggregate[None, :], ((0, HEAD - 3), (0, LANES - rows))),
        ],
        axis=0,
    )
    meta = jnp.concatenate([head, place], axis=0)
    bf16, f32 = jnp.bfloat16, jnp.float32
    tall = rows * width
    side = listed * width
    scratch = [
        pltpu.VMEM((rows, slots + 1, width, width), bf16),
        pltpu.VMEM((rows, width, width), bf16),
        pltpu.VMEM((rows, width, width), bf16),
        pltpu.VMEM((tall, tall), bf16),
        pltpu.VMEM((2, tall, side), bf16),
        pltpu.VMEM((tall, span), bf16),
        pltpu.VMEM((2, listed, width, width), bf16),
        pltpu.VMEM((2, listed, width, width), bf16),
        pltpu.VMEM((2, HEAD, LANES), jnp.int32),
        pltpu.SMEM((2, HEAD, LANES), jnp.int32),
        pltpu.VMEM((2, side, span), bf16),
        pltpu.VMEM((3, rows, width, span), bf16),
        pltpu.VMEM((2, 3, side, span), bf16),
        pltpu.VMEM((2, 3, side, span), bf16),
        pltpu.VMEM((3, rows, span, width), bf16),
        pltpu.VMEM((tall, span), bf16),
        pltpu.VMEM((5, span, span), f32),
        pltpu.VMEM((2, 5, span, span), bf16),
        pltpu.VMEM((2, 5, span, span), bf16),
        pltpu.VMEM((7, CA, width, span), bf16),
        pltpu.SemaphoreType.DMA((rows,)),
        pltpu.SemaphoreType.DMA((4,)),
        pltpu.SemaphoreType.DMA((7,)),
        pltpu.SemaphoreType.DMA((2, MESSAGES)),
        pltpu.SemaphoreType.DMA((2, MESSAGES)),
    ]
    flops = 2 * tall * span * (tall * 4 + side * 8 + 15 * span)
    return pl.pallas_call(
        functools.partial(kernel, n_grp, n_dev),
        out_shape=jax.ShapeDtypeStruct((CA, width, 7 * span), bf16),
        in_specs=[
            pl.BlockSpec(memory_space=pltpu.SMEM),
            pl.BlockSpec(memory_space=pltpu.SMEM),
            pl.BlockSpec(memory_space=pltpu.VMEM),
            pl.BlockSpec(memory_space=pl.ANY),
            pl.BlockSpec(memory_space=pl.ANY),
            pl.BlockSpec(memory_space=pl.ANY),
        ],
        out_specs=pl.BlockSpec(memory_space=pl.ANY),
        scratch_shapes=scratch,
        compiler_params=pltpu.CompilerParams(
            collective_id=0, has_side_effects=True, vmem_limit_bytes=48 << 20
        ),
        cost_estimate=pl.CostEstimate(
            flops=flops, bytes_accessed=block_values.size * 2, transcendentals=0
        ),
    )(damping, meta, meta, block_values, tentative, inverse_diagonal)


def solution(mesh):
    return jax.shard_map(
        functools.partial(shards, mesh.shape["grp"], mesh.shape["dev"]),
        mesh=mesh,
        in_specs=(
            P(("grp", "dev"), None, None, None),
            P(("grp", "dev"), None),
            P(("grp", "dev"), None, None),
            P(("grp", "dev"), None, None),
            P(("grp", "dev")),
            P(("grp", "dev"), None, None),
            P(),
        ),
        out_specs=P(("grp", "dev"), None, None),
        check_vma=False,
    )
```

```python
import functools

import jax
import jax.numpy as jnp
from jax import lax
from jax.experimental import pallas as pl
from jax.experimental.pallas import tpu as pltpu
from jax.sharding import PartitionSpec as P

CA = 2
HEAD = 8
LANES = 128
META, TENT, MID, LEFT, RIGHT, PART = 0, 1, 2, 3, 4, 5
MESSAGES = 10


def dot(a, b):
    return jnp.dot(a, b, preferred_element_type=jnp.float32)


def kernel(
    n_grp,
    n_dev,
    damping_ref,
    columns_ref,
    aggregate_ref,
    ghost_ref,
    values_hbm,
    tent_hbm,
    inv_hbm,
    out_hbm,
    meta_vec,
    meta_ref,
    a_raw,
    t_raw,
    d_raw,
    a_own,
    a_side,
    tt,
    stage_t,
    ghost_t,
    meta_in,
    meta_s,
    tg,
    p,
    stage_p,
    ghost_p,
    pt,
    ap,
    own_acc,
    part_send,
    part_recv,
    out_v,
    a_sem,
    local_sem,
    out_sem,
    send_sem,
    recv_sem,
):
    rows, slots, width, _ = values_hbm.shape
    listed = stage_t.shape[1]
    span = CA * width
    group = max(g for g in (1, 2, 3, 4) if rows % g == 0)
    chunk = group * width
    total = n_grp * n_dev
    me = lax.axis_index("grp") * n_dev + lax.axis_index("dev")
    has = (me > 0, me < total - 1)
    other = (lax.rem(me + (total - 1), total), lax.rem(me + 1, total))
    device = [(lax.div(o, n_dev), lax.rem(o, n_dev)) for o in other]

    def message(side, index, source, target):
        return pltpu.make_async_remote_copy(
            src_ref=source,
            dst_ref=target,
            send_sem=send_sem.at[side, index],
            recv_sem=recv_sem.at[1 - side, index],
            device_id=device[side],
            device_id_type=pl.DeviceIdType.MESH,
        )

    def meta_msg(side):
        return message(side, META, meta_vec.at[pl.ds(0, HEAD)], meta_in.at[1 - side])

    def tent_msg(side):
        return message(side, TENT, stage_t.at[side], ghost_t.at[1 - side])

    def p_msg(side, part):
        index = (LEFT, MID, RIGHT)[part]
        return message(side, index, stage_p.at[side, part], ghost_p.at[1 - side, part])

    def part_msg(side, column):
        return message(
            side, PART + column, part_send.at[side, column], part_recv.at[1 - side, column]
        )

    def both(action):
        for side in (0, 1):
            pl.when(has[side])(functools.partial(action, side))

    barrier = pltpu.get_barrier_semaphore()
    both(
        lambda side: pl.semaphore_signal(
            barrier, inc=1, device_id=device[side], device_id_type=pl.DeviceIdType.MESH
        )
    )

    def a_copy(r):
        return pltpu.make_async_copy(
            values_hbm.at[r], a_raw.at[r, pl.ds(0, slots)], a_sem.at[r]
        )

    t_copy = pltpu.make_async_copy(tent_hbm, t_raw, local_sem.at[0])
    d_copy = pltpu.make_async_copy(inv_hbm, d_raw, local_sem.at[1])
    t_copy.start()

    @pl.loop(0, rows)
    def _(r):
        a_copy(r).start()
        a_raw[r, slots] = jnp.zeros((width, width), a_raw.dtype)

    d_copy.start()
    lane = lax.broadcasted_iota(jnp.int32, (rows, LANES), 1)
    place = jnp.full((rows, LANES), slots, jnp.int32)
    for k in range(slots):
        place = jnp.where(columns_ref[:, k : k + 1] == lane, k, place)
    meta_vec[0:2, 0:listed] = ghost_ref[...]
    meta_vec[2:3, 0:rows] = aggregate_ref[...]
    meta_vec[HEAD : HEAD + rows, :] = place
    m_copy = pltpu.make_async_copy(meta_vec, meta_ref, local_sem.at[4])
    m_copy.start()
    for side in (0, 1):

        @pl.when(jnp.logical_not(has[side]))
        def _():
            tg[side] = jnp.zeros(tg.shape[1:], tg.dtype)
            ghost_p[side] = jnp.zeros(ghost_p.shape[1:], ghost_p.dtype)
            part_recv[side] = jnp.zeros(part_recv.shape[1:], part_recv.dtype)

    pl.semaphore_wait(barrier, has[0].astype(jnp.int32) + has[1].astype(jnp.int32))
    both(lambda side: meta_msg(side).start())

    def placed(block, coarse):
        wide = jnp.concatenate([block] * CA, axis=1)
        at = lax.broadcasted_iota(jnp.int32, wide.shape, 1) // width
        return jnp.where(at == jnp.full(wide.shape, coarse, jnp.int32), wide, 0).astype(block.dtype)

    t_copy.wait()
    m_copy.wait()

    @pl.loop(0, rows)
    def _(r):
        tt[pl.ds(pl.multiple_of(r * width, width), width), :] = placed(t_raw[r], meta_ref[2, r])

    def lists_in(side):
        meta_msg(1 - side).wait_recv()
        copy = pltpu.make_async_copy(meta_in.at[side], meta_s.at[side], local_sem.at[2 + side])
        copy.start()
        copy.wait()
        for s in range(listed):
            stage_t[side, s] = t_raw[meta_s[side, 1 - side, s]]
        tent_msg(side).start()

    both(lists_in)

    @pl.loop(0, rows)
    def _(r):
        a_copy(r).wait()

    @pl.loop(0, rows)
    def _(r):
        at = pl.ds(pl.multiple_of(r * width, width), width)
        for l in range(rows):
            a_own[at, l * width : (l + 1) * width] = a_raw[r, meta_ref[HEAD + r, l]]
        for side in (0, 1):
            for s in range(listed):
                a_side[side, at, s * width : (s + 1) * width] = a_raw[
                    r, meta_ref[HEAD + r, rows + side * listed + s]
                ]

    d_copy.wait()
    damping = damping_ref[0]

    def smooth(part, matrix, lookup, keep):
        @pl.loop(0, rows // group)
        def _(g):
            at = pl.ds(pl.multiple_of(g * chunk, chunk), chunk)
            half = dot(matrix[at, :], lookup[...]).astype(jnp.bfloat16)
            for i in range(group):
                r = g * group + i
                here = pl.ds(pl.multiple_of(r * width, width), width)
                scaled = damping * dot(d_raw[r], half[i * width : (i + 1) * width])
                if keep:
                    value = tt[here, :].astype(jnp.float32) - scaled
                else:
                    value = -scaled
                p[part, r] = value.astype(jnp.bfloat16)

    def send_p(part):
        def send(side):
            for s in range(listed):
                stage_p[side, part, s * width : (s + 1) * width, :] = p[
                    part, meta_s[side, 1 - side, s]
                ]
            p_msg(side, part).start()

        both(send)

    smooth(1, a_own, tt, True)
    send_p(1)

    def tent_in(side):
        tent_msg(1 - side).wait_recv()
        for s in range(listed):
            coarse = meta_s[side, 2, meta_ref[side, s]]
            tg[side, s * width : (s + 1) * width, :] = placed(ghost_t[side, s], coarse)

    both(tent_in)
    smooth(0, a_side.at[0], tg.at[0], False)
    send_p(0)
    smooth(2, a_side.at[1], tg.at[1], False)
    send_p(2)

    for part in range(3):

        @pl.loop(0, rows)
        def _(r):
            pt[part, r] = p[part, r].T

    def galerkin(column, terms):
        @pl.loop(0, rows // group)
        def _(g):
            at = pl.ds(pl.multiple_of(g * chunk, chunk), chunk)
            value = None
            for matrix, lookup in terms:
                term = dot(matrix[at, :], lookup[...].reshape(-1, span))
                value = term if value is None else value + term
            ap[at, :] = value.astype(jnp.bfloat16)

        def product(part):
            lhs = jnp.concatenate([pt[part, r] for r in range(rows)], axis=1)
            return dot(lhs, ap[...])

        for side, part in ((0, 0), (1, 2)):
            part_send[side, column] = product(part).astype(jnp.bfloat16)
            pl.when(has[side])(lambda: part_msg(side, column).start())
        own_acc[column] = product(1)

    def p_in(side, part):
        pl.when(has[side])(lambda: p_msg(1 - side, part).wait_recv())

    left, right = a_side.at[0], a_side.at[1]
    p_in(0, 1)
    galerkin(1, [(a_own, p.at[0]), (left, ghost_p.at[0, 1])])
    p_in(1, 1)
    galerkin(3, [(a_own, p.at[2]), (right, ghost_p.at[1, 1])])
    p_in(0, 0)
    galerkin(0, [(left, ghost_p.at[0, 0])])
    p_in(1, 2)
    galerkin(4, [(right, ghost_p.at[1, 2])])
    p_in(0, 2)
    p_in(1, 0)
    galerkin(2, [(a_own, p.at[1]), (left, ghost_p.at[0, 2]), (right, ghost_p.at[1, 0])])

    def out_copy(s):
        return pltpu.make_async_copy(
            out_v.at[s], out_hbm.at[:, :, pl.ds(s * span, span)], out_sem.at[s]
        )

    for s in (1, 5, 3, 0, 6, 2, 4):
        value = None
        if 0 <= s - 1 < 5:
            value = own_acc[s - 1]
        for side, column in ((0, s), (1, s - 2)):
            if 0 <= column < 5:
                pl.when(has[side])(lambda: part_msg(1 - side, column).wait_recv())
                term = part_recv[side, column].astype(jnp.float32)
                value = term if value is None else value + term
        out_v[s] = value.astype(jnp.bfloat16).reshape(CA, width, span)
        out_copy(s).start()

    def finish(side):
        meta_msg(side).wait_send()
        tent_msg(side).wait_send()
        for part in range(3):
            p_msg(side, part).wait_send()
        for column in range(5):
            part_msg(side, column).wait_send()

    both(finish)
    for s in range(7):
        out_copy(s).wait()


def shards(
    n_grp,
    n_dev,
    block_values,
    block_columns,
    tentative,
    inverse_diagonal,
    aggregate,
    ghost_rows,
    damping,
):
    rows, slots = block_columns.shape
    width = tentative.shape[1]
    listed = ghost_rows.shape[2]
    span = CA * width
    bf16, f32 = jnp.bfloat16, jnp.float32
    tall = rows * width
    side = listed * width
    scratch = [
        pltpu.VMEM((HEAD + rows, LANES), jnp.int32),
        pltpu.SMEM((HEAD + rows, LANES), jnp.int32),
        pltpu.VMEM((rows, slots + 1, width, width), bf16),
        pltpu.VMEM((rows, width, width), bf16),
        pltpu.VMEM((rows, width, width), bf16),
        pltpu.VMEM((tall, tall), bf16),
        pltpu.VMEM((2, tall, side), bf16),
        pltpu.VMEM((tall, span), bf16),
        pltpu.VMEM((2, listed, width, width), bf16),
        pltpu.VMEM((2, listed, width, width), bf16),
        pltpu.VMEM((2, HEAD, LANES), jnp.int32),
        pltpu.SMEM((2, HEAD, LANES), jnp.int32),
        pltpu.VMEM((2, side, span), bf16),
        pltpu.VMEM((3, rows, width, span), bf16),
        pltpu.VMEM((2, 3, side, span), bf16),
        pltpu.VMEM((2, 3, side, span), bf16),
        pltpu.VMEM((3, rows, span, width), bf16),
        pltpu.VMEM((tall, span), bf16),
        pltpu.VMEM((5, span, span), f32),
        pltpu.VMEM((2, 5, span, span), bf16),
        pltpu.VMEM((2, 5, span, span), bf16),
        pltpu.VMEM((7, CA, width, span), bf16),
        pltpu.SemaphoreType.DMA((rows,)),
        pltpu.SemaphoreType.DMA((5,)),
        pltpu.SemaphoreType.DMA((7,)),
        pltpu.SemaphoreType.DMA((2, MESSAGES)),
        pltpu.SemaphoreType.DMA((2, MESSAGES)),
    ]
    flops = 2 * tall * span * (tall * 4 + side * 8 + 15 * span)
    return pl.pallas_call(
        functools.partial(kernel, n_grp, n_dev),
        out_shape=jax.ShapeDtypeStruct((CA, width, 7 * span), bf16),
        in_specs=[
            pl.BlockSpec(memory_space=pltpu.SMEM),
            pl.BlockSpec(memory_space=pltpu.VMEM),
            pl.BlockSpec(memory_space=pltpu.VMEM),
            pl.BlockSpec(memory_space=pltpu.VMEM),
            pl.BlockSpec(memory_space=pl.ANY),
            pl.BlockSpec(memory_space=pl.ANY),
            pl.BlockSpec(memory_space=pl.ANY),
        ],
        out_specs=pl.BlockSpec(memory_space=pl.ANY),
        scratch_shapes=scratch,
        compiler_params=pltpu.CompilerParams(
            collective_id=0, has_side_effects=True, vmem_limit_bytes=60 << 20
        ),
        cost_estimate=pl.CostEstimate(
            flops=flops, bytes_accessed=block_values.size * 2, transcendentals=0
        ),
    )(
        damping,
        block_columns,
        aggregate[None, :],
        ghost_rows[0],
        block_values,
        tentative,
        inverse_diagonal,
    )


def solution(mesh):
    return jax.shard_map(
        functools.partial(shards, mesh.shape["grp"], mesh.shape["dev"]),
        mesh=mesh,
        in_specs=(
            P(("grp", "dev"), None, None, None),
            P(("grp", "dev"), None),
            P(("grp", "dev"), None, None),
            P(("grp", "dev"), None, None),
            P(("grp", "dev")),
            P(("grp", "dev"), None, None),
            P(),
        ),
        out_specs=P(("grp", "dev"), None, None),
        check_vma=False,
    )
```

```python
import functools

import jax
import jax.numpy as jnp
from jax import lax
from jax.experimental import pallas as pl
from jax.experimental.pallas import tpu as pltpu
from jax.sharding import PartitionSpec as P

CA = 2
HEAD = 8
LANES = 128
META, TENT, MID, LEFT, RIGHT, PART = 0, 1, 2, 3, 4, 5
MESSAGES = 10


def dot(a, b):
    return jnp.dot(a, b, preferred_element_type=jnp.float32)


def kernel(
    n_grp,
    n_dev,
    damping_ref,
    columns_ref,
    aggregate_ref,
    ghost_ref,
    values_hbm,
    tent_hbm,
    inv_hbm,
    out_hbm,
    meta_vec,
    meta_ref,
    a_raw,
    t_raw,
    d_raw,
    a_own,
    a_side,
    tt,
    stage_t,
    ghost_t,
    meta_in,
    meta_s,
    tg,
    p,
    stage_p,
    ghost_p,
    pt,
    ap,
    base,
    own_acc,
    part_send,
    part_recv,
    out_v,
    a_sem,
    local_sem,
    out_sem,
    send_sem,
    recv_sem,
):
    rows, slots, width, _ = values_hbm.shape
    listed = stage_t.shape[1]
    span = CA * width
    group = max(g for g in (1, 2, 3, 4) if rows % g == 0)
    chunk = group * width
    total = n_grp * n_dev
    me = lax.axis_index("grp") * n_dev + lax.axis_index("dev")
    has = (me > 0, me < total - 1)
    other = (lax.rem(me + (total - 1), total), lax.rem(me + 1, total))
    device = [(lax.div(o, n_dev), lax.rem(o, n_dev)) for o in other]

    def message(side, index, source, target):
        return pltpu.make_async_remote_copy(
            src_ref=source,
            dst_ref=target,
            send_sem=send_sem.at[side, index],
            recv_sem=recv_sem.at[1 - side, index],
            device_id=device[side],
            device_id_type=pl.DeviceIdType.MESH,
        )

    def meta_msg(side):
        return message(side, META, meta_vec.at[pl.ds(0, HEAD)], meta_in.at[1 - side])

    def tent_msg(side):
        return message(side, TENT, stage_t.at[side], ghost_t.at[1 - side])

    def p_msg(side, part):
        index = (LEFT, MID, RIGHT)[part]
        return message(side, index, stage_p.at[side, part], ghost_p.at[1 - side, part])

    def part_msg(side, column):
        return message(
            side, PART + column, part_send.at[side, column], part_recv.at[1 - side, column]
        )

    def both(action):
        for side in (0, 1):
            pl.when(has[side])(functools.partial(action, side))

    barrier = pltpu.get_barrier_semaphore()
    both(
        lambda side: pl.semaphore_signal(
            barrier, inc=1, device_id=device[side], device_id_type=pl.DeviceIdType.MESH
        )
    )

    def a_copy(r):
        return pltpu.make_async_copy(
            values_hbm.at[r], a_raw.at[r, pl.ds(0, slots)], a_sem.at[r]
        )

    t_copy = pltpu.make_async_copy(tent_hbm, t_raw, local_sem.at[0])
    d_copy = pltpu.make_async_copy(inv_hbm, d_raw, local_sem.at[1])
    t_copy.start()

    @pl.loop(0, rows)
    def _(r):
        a_copy(r).start()
        a_raw[r, slots] = jnp.zeros((width, width), a_raw.dtype)

    d_copy.start()
    lane = lax.broadcasted_iota(jnp.int32, (rows, LANES), 1)
    place = jnp.full((rows, LANES), slots, jnp.int32)
    for k in range(slots):
        place = jnp.where(columns_ref[:, k : k + 1] == lane, k, place)
    meta_vec[0:2, 0:listed] = ghost_ref[...]
    meta_vec[2:3, 0:rows] = aggregate_ref[...]
    meta_vec[HEAD : HEAD + rows, :] = place
    m_copy = pltpu.make_async_copy(meta_vec, meta_ref, local_sem.at[4])
    m_copy.start()
    for side in (0, 1):

        @pl.when(jnp.logical_not(has[side]))
        def _():
            tg[side] = jnp.zeros(tg.shape[1:], tg.dtype)
            ghost_p[side] = jnp.zeros(ghost_p.shape[1:], ghost_p.dtype)
            part_recv[side] = jnp.zeros(part_recv.shape[1:], part_recv.dtype)

    pl.semaphore_wait(barrier, has[0].astype(jnp.int32) + has[1].astype(jnp.int32))
    both(lambda side: meta_msg(side).start())

    def placed(block, coarse):
        wide = jnp.concatenate([block] * CA, axis=1)
        at = lax.broadcasted_iota(jnp.int32, wide.shape, 1) // width
        return jnp.where(at == jnp.full(wide.shape, coarse, jnp.int32), wide, 0).astype(block.dtype)

    t_copy.wait()
    m_copy.wait()

    @pl.loop(0, rows)
    def _(r):
        tt[pl.ds(pl.multiple_of(r * width, width), width), :] = placed(t_raw[r], meta_ref[2, r])

    @pl.loop(0, rows)
    def _(r):
        a_copy(r).wait()

    @pl.loop(0, rows)
    def _(r):
        at = pl.ds(pl.multiple_of(r * width, width), width)
        for l in range(rows):
            a_own[at, l * width : (l + 1) * width] = a_raw[r, meta_ref[HEAD + r, l]]
        for side in (0, 1):
            for s in range(listed):
                a_side[side, at, s * width : (s + 1) * width] = a_raw[
                    r, meta_ref[HEAD + r, rows + side * listed + s]
                ]

    def lists_in(side):
        meta_msg(1 - side).wait_recv()
        copy = pltpu.make_async_copy(meta_in.at[side], meta_s.at[side], local_sem.at[2 + side])
        copy.start()
        copy.wait()
        for s in range(listed):
            stage_t[side, s] = t_raw[meta_s[side, 1 - side, s]]
        tent_msg(side).start()

    both(lists_in)

    d_copy.wait()
    damping = damping_ref[...]

    def smooth(part, matrix, lookup, keep):
        @pl.loop(0, rows // group)
        def _(g):
            at = pl.ds(pl.multiple_of(g * chunk, chunk), chunk)
            half = dot(matrix[at, :], lookup[...]).astype(jnp.bfloat16)
            for i in range(group):
                r = g * group + i
                here = pl.ds(pl.multiple_of(r * width, width), width)
                scaled = damping * dot(d_raw[r], half[i * width : (i + 1) * width])
                if keep:
                    value = tt[here, :].astype(jnp.float32) - scaled
                else:
                    value = -scaled
                p[part, r] = value.astype(jnp.bfloat16)

    def send_p(part):
        def send(side):
            for s in range(listed):
                stage_p[side, part, s * width : (s + 1) * width, :] = p[
                    part, meta_s[side, 1 - side, s]
                ]
            p_msg(side, part).start()

        both(send)

    smooth(1, a_own, tt, True)
    send_p(1)

    def tent_in(side):
        tent_msg(1 - side).wait_recv()
        for s in range(listed):
            coarse = meta_s[side, 2, meta_ref[side, s]]
            tg[side, s * width : (s + 1) * width, :] = placed(ghost_t[side, s], coarse)

    both(tent_in)
    smooth(0, a_side.at[0], tg.at[0], False)
    send_p(0)
    smooth(2, a_side.at[1], tg.at[1], False)
    send_p(2)

    for part in range(3):

        @pl.loop(0, rows)
        def _(r):
            pt[part, r] = p[part, r].T

    def ahead(column, part):
        @pl.loop(0, rows // group)
        def _(g):
            at = pl.ds(pl.multiple_of(g * chunk, chunk), chunk)
            base[column - 1, at, :] = dot(a_own[at, :], p[part].reshape(-1, span))

    def galerkin(column, terms):
        @pl.loop(0, rows // group)
        def _(g):
            at = pl.ds(pl.multiple_of(g * chunk, chunk), chunk)
            value = base[column - 1, at, :] if 1 <= column <= 3 else None
            for matrix, lookup in terms:
                term = dot(matrix[at, :], lookup[...])
                value = term if value is None else value + term
            ap[at, :] = value.astype(jnp.bfloat16)

        def product(part):
            lhs = jnp.concatenate([pt[part, r] for r in range(rows)], axis=1)
            return dot(lhs, ap[...])

        for side, part in ((0, 0), (1, 2)):
            part_send[side, column] = product(part).astype(jnp.bfloat16)
            pl.when(has[side])(lambda: part_msg(side, column).start())
        own_acc[column] = product(1)

    def p_in(side, part):
        pl.when(has[side])(lambda: p_msg(1 - side, part).wait_recv())

    left, right = a_side.at[0], a_side.at[1]
    ahead(1, 0)
    ahead(3, 2)
    p_in(0, 1)
    galerkin(1, [(left, ghost_p.at[0, 1])])
    p_in(1, 1)
    galerkin(3, [(right, ghost_p.at[1, 1])])
    ahead(2, 1)
    p_in(0, 0)
    galerkin(0, [(left, ghost_p.at[0, 0])])
    p_in(1, 2)
    galerkin(4, [(right, ghost_p.at[1, 2])])
    p_in(0, 2)
    p_in(1, 0)
    galerkin(2, [(left, ghost_p.at[0, 2]), (right, ghost_p.at[1, 0])])

    def out_copy(s):
        return pltpu.make_async_copy(
            out_v.at[s], out_hbm.at[:, :, pl.ds(s * span, span)], out_sem.at[s]
        )

    for s in (1, 5, 3, 0, 6, 2, 4):
        value = None
        if 0 <= s - 1 < 5:
            value = own_acc[s - 1]
        for side, column in ((0, s), (1, s - 2)):
            if 0 <= column < 5:
                pl.when(has[side])(lambda: part_msg(1 - side, column).wait_recv())
                term = part_recv[side, column].astype(jnp.float32)
                value = term if value is None else value + term
        out_v[s] = value.astype(jnp.bfloat16).reshape(CA, width, span)
        out_copy(s).start()

    def finish(side):
        meta_msg(side).wait_send()
        tent_msg(side).wait_send()
        for part in range(3):
            p_msg(side, part).wait_send()
        for column in range(5):
            part_msg(side, column).wait_send()

    both(finish)
    for s in range(7):
        out_copy(s).wait()


def shards(
    n_grp,
    n_dev,
    block_values,
    block_columns,
    tentative,
    inverse_diagonal,
    aggregate,
    ghost_rows,
    damping,
):
    rows, slots = block_columns.shape
    width = tentative.shape[1]
    listed = ghost_rows.shape[2]
    span = CA * width
    bf16, f32 = jnp.bfloat16, jnp.float32
    tall = rows * width
    side = listed * width
    scratch = [
        pltpu.VMEM((HEAD + rows, LANES), jnp.int32),
        pltpu.SMEM((HEAD + rows, LANES), jnp.int32),
        pltpu.VMEM((rows, slots + 1, width, width), bf16),
        pltpu.VMEM((rows, width, width), bf16),
        pltpu.VMEM((rows, width, width), bf16),
        pltpu.VMEM((tall, tall), bf16),
        pltpu.VMEM((2, tall, side), bf16),
        pltpu.VMEM((tall, span), bf16),
        pltpu.VMEM((2, listed, width, width), bf16),
        pltpu.VMEM((2, listed, width, width), bf16),
        pltpu.VMEM((2, HEAD, LANES), jnp.int32),
        pltpu.SMEM((2, HEAD, LANES), jnp.int32),
        pltpu.VMEM((2, side, span), bf16),
        pltpu.VMEM((3, rows, width, span), bf16),
        pltpu.VMEM((2, 3, side, span), bf16),
        pltpu.VMEM((2, 3, side, span), bf16),
        pltpu.VMEM((3, rows, span, width), bf16),
        pltpu.VMEM((tall, span), bf16),
        pltpu.VMEM((3, tall, span), f32),
        pltpu.VMEM((5, span, span), f32),
        pltpu.VMEM((2, 5, span, span), bf16),
        pltpu.VMEM((2, 5, span, span), bf16),
        pltpu.VMEM((7, CA, width, span), bf16),
        pltpu.SemaphoreType.DMA((rows,)),
        pltpu.SemaphoreType.DMA((5,)),
        pltpu.SemaphoreType.DMA((7,)),
        pltpu.SemaphoreType.DMA((2, MESSAGES)),
        pltpu.SemaphoreType.DMA((2, MESSAGES)),
    ]
    flops = 2 * tall * span * (tall * 4 + side * 8 + 15 * span)
    return pl.pallas_call(
        functools.partial(kernel, n_grp, n_dev),
        out_shape=jax.ShapeDtypeStruct((CA, width, 7 * span), bf16),
        in_specs=[
            pl.BlockSpec(memory_space=pltpu.VMEM),
            pl.BlockSpec(memory_space=pltpu.VMEM),
            pl.BlockSpec(memory_space=pltpu.VMEM),
            pl.BlockSpec(memory_space=pltpu.VMEM),
            pl.BlockSpec(memory_space=pl.ANY),
            pl.BlockSpec(memory_space=pl.ANY),
            pl.BlockSpec(memory_space=pl.ANY),
        ],
        out_specs=pl.BlockSpec(memory_space=pl.ANY),
        scratch_shapes=scratch,
        compiler_params=pltpu.CompilerParams(
            collective_id=0, has_side_effects=True, vmem_limit_bytes=60 << 20
        ),
        cost_estimate=pl.CostEstimate(
            flops=flops, bytes_accessed=block_values.size * 2, transcendentals=0
        ),
    )(
        damping[None, :],
        block_columns,
        aggregate[None, :],
        ghost_rows[0],
        block_values,
        tentative,
        inverse_diagonal,
    )


def solution(mesh):
    return jax.shard_map(
        functools.partial(shards, mesh.shape["grp"], mesh.shape["dev"]),
        mesh=mesh,
        in_specs=(
            P(("grp", "dev"), None, None, None),
            P(("grp", "dev"), None),
            P(("grp", "dev"), None, None),
            P(("grp", "dev"), None, None),
            P(("grp", "dev")),
            P(("grp", "dev"), None, None),
            P(),
        ),
        out_specs=P(("grp", "dev"), None, None),
        check_vma=False,
    )
```
